512 devices in a mesh: chain: 16 (over y, core), sector: 32 (over x, z).
Axes of the slice: x: 4, y: 8, z: 8, core: 2. Of those that a mesh axis runs over, the one named last changes fastest.
Arguments:
- left_sites: bfloat16 [16, 32, 256, 6, 256], P('chain', 'sector'), may hold values from -0.375 to 0.375
- right_sites: bfloat16 [16, 32, 256, 6, 256], P('chain', 'sector'), may hold values from -6 to 6
- pair_gates: bfloat16 [16, 36, 36], P('chain'), as said below
- test_matrix: bfloat16 [16, 32, 1536, 256], P('chain', 'sector'), may hold values from -0.15625 to 0.15625
- kept_columns: int32 [16, 32], P('chain', 'sector'), may hold values from 32 to 256, as said below
Outputs:
- new_left: bfloat16 [16, 32, 256, 6, 256], P('chain', 'sector')
- new_right: bfloat16 [16, 32, 256, 6, 256], P('chain', 'sector')
The draws below stay inside these ranges and needn't reach their ends.
Inputs may be any that keep to these rules, and one draw needn't show every extreme that they name: pair_gates[c, p * 6 + q, n * 6 + r] is zero unless p + q = n + r. `kept_columns`: every bond has a sector that keeps all 256 columns.
All inputs are finite; a program needn't handle non-finite values.
Results may differ from the reference program's by a relative error of at most 0.0063.
Values may be sent and summed in bfloat16 or wider, within the bound.
A program may use at most 64 MiB of HBM per device.

```python
import math
import jax
import jax.numpy as jnp
from jax import lax

D = 6
S = 256
PAIRS = 16
SECTORS = 32


def draw_pair_gates(key, part):
    key = jax.random.fold_in(key, 11)
    states = D * D
    indices = jnp.arange(states, dtype=jnp.int32)
    totals = indices // D + indices % D
    same_total = totals[:, None] == totals[None, :]
    counts = jnp.minimum(totals, 2 * D - 2 - totals) + 1
    spread = 0.6 / jnp.sqrt(counts.astype(jnp.float32))
    noise = jax.random.normal(key, (PAIRS, states, states), jnp.float32)
    identity = jnp.eye(states, dtype=jnp.float32)
    values = 0.8 * identity[None] + noise * spread[None, None, :]
    return jnp.where(same_total[None], values, 0.0).astype(jnp.bfloat16)


def draw_kept_columns(key, part):
    key = jax.random.fold_in(key, 23)
    first_key, second_key = jax.random.split(key)
    counts = jax.random.randint(first_key, (PAIRS, SECTORS), S // 8, S + 1, dtype=jnp.int32)
    chosen = jax.random.randint(second_key, (PAIRS, 1), 0, SECTORS, dtype=jnp.int32)
    column = jnp.arange(SECTORS, dtype=jnp.int32)[None, :]
    return jnp.where(column == chosen, S, counts).astype(jnp.int32)


def block_scale(own_key, shape, shards, low, largest):
    def one(dim, shards_of):
        heights = jax.random.uniform(jax.random.fold_in(jax.random.fold_in(own_key, 6), dim), (shards_of,), jnp.float32, low / len(shards), largest / len(shards))
        return jnp.repeat(jnp.exp(heights), shape[dim] // shards_of).reshape((-1,) + (1,) * (len(shape) - dim - 1))

    gain = one(*shards[0])
    for cut in shards[1:]:
        gain = gain * one(*cut)
    return gain


def normal_values(rng, extent, width, bound, cuts=(), kind=jnp.bfloat16):
    factor_of = block_scale(rng, extent, cuts, -0.22, 0.18) if cuts else 1.0
    array = jax.random.normal(rng, extent, jnp.float32) * width * factor_of
    return jnp.minimum(jnp.maximum(array, -bound), bound).astype(kind)


def setup_inputs(seed: int = 0) -> dict:
    key_list = jax.random.split(jax.random.key(seed), 6)
    left_sites = normal_values(key_list[0], (PAIRS, SECTORS, S, D, S), S ** -0.5, 0.375, ((0, 16), (1, 32)))
    right_sites = normal_values(key_list[1], (PAIRS, SECTORS, S, D, S), 1.0, 6.0, ((0, 16), (1, 32)))
    pair_gates = draw_pair_gates(jax.random.fold_in(key_list[5], 71), 0)
    test_matrix = normal_values(key_list[3], (PAIRS, SECTORS, D * S, S), (D * S) ** -0.5, 0.15625, ((0, 16), (1, 32)))
    kept_columns = draw_kept_columns(jax.random.fold_in(key_list[5], 71), 0)
    return {"left_sites": left_sites, "right_sites": right_sites, "pair_gates": pair_gates, "test_matrix": test_matrix, "kept_columns": kept_columns}


RIDGE_SHARE = 0.05
TINY_SHIFT = 1e-05

def mix_blocks(left_pair, right_pair, gate_pair):
    gate_full = gate_pair.astype(jnp.float32)
    photon_axis = jnp.arange(D, dtype=jnp.int32)

    def one_left(left_sector):
        left_rows = lax.dynamic_index_in_dim(left_pair, left_sector, 0, keepdims=False).astype(jnp.float32)
        partials = []
        for first_level in range(D):
            middle = left_sector + first_level
            partner = lax.dynamic_index_in_dim(right_pair, jnp.minimum(middle, SECTORS - 1).astype(jnp.int32), 0, keepdims=False)
            partner = partner.astype(jnp.float32).reshape(S, D * S)
            middle_live = (middle < SECTORS).astype(jnp.float32)
            partial_value = jnp.dot(left_rows[:, first_level, :].astype(jnp.float32), partner.astype(jnp.float32), preferred_element_type=jnp.float32).reshape(S, D, S)
            right_live = (left_sector + first_level + photon_axis < SECTORS).astype(jnp.float32) * middle_live
            partials.append((partial_value * right_live[None, :, None]).astype(jnp.bfloat16))
        product = jnp.stack(partials, axis=1).reshape(S, D * D, S).astype(jnp.float32)
        mixed = jnp.einsum('xy,iyk->ixk', gate_full, product)
        return mixed.reshape(S, D, D, S).astype(jnp.bfloat16)
    return lax.map(one_left, jnp.arange(SECTORS, dtype=jnp.int32))

def orthonormal_basis(stacked, sketch_in, kept_count):
    stacked_full = stacked.astype(jnp.float32)
    first_sketch = jnp.dot(stacked_full.astype(jnp.float32), sketch_in.astype(jnp.float32), preferred_element_type=jnp.float32).astype(jnp.bfloat16)
    back_sketch = jnp.einsum('rk,rc->kc', stacked_full, first_sketch.astype(jnp.float32)).astype(jnp.bfloat16)
    sketch = jnp.dot(stacked_full.astype(jnp.float32), back_sketch.astype(jnp.float32), preferred_element_type=jnp.float32)
    gram_matrix = jnp.einsum('rc,rd->cd', sketch, sketch, precision=lax.Precision.HIGHEST)
    ridge_term = RIDGE_SHARE * jnp.trace(gram_matrix) / S + TINY_SHIFT
    gram_matrix = gram_matrix + ridge_term * jnp.eye(S, dtype=jnp.float32)
    factor = jnp.linalg.cholesky(gram_matrix)
    basis_cols = jax.scipy.linalg.solve_triangular(factor, sketch.T, lower=True).T
    column = jnp.arange(S, dtype=jnp.int32)
    return jnp.where(column[None, :] < kept_count, basis_cols, 0.0)

def bond_update(left_pair, right_pair, gate_pair, sketch_pair, kept_pair):
    mixed_all = mix_blocks(left_pair, right_pair, gate_pair)
    basis_scale = math.sqrt(D * S)

    def one_middle(middle_sector):
        row_blocks = []
        for photon in range(D):
            source = middle_sector - photon
            source_block = lax.dynamic_index_in_dim(mixed_all, jnp.maximum(source, 0).astype(jnp.int32), 0, keepdims=False)[:, photon]
            row_blocks.append(jnp.where(source >= 0, source_block, jnp.zeros_like(source_block)))
        stacked = jnp.stack(row_blocks, axis=0).reshape(D * S, D * S)
        sketch_in = lax.dynamic_index_in_dim(sketch_pair, middle_sector, 0, keepdims=False)
        kept_count = lax.dynamic_index_in_dim(kept_pair, middle_sector, 0, keepdims=False)
        basis_cols = orthonormal_basis(stacked, sketch_in, kept_count)
        scaled = (basis_cols * basis_scale).astype(jnp.bfloat16)
        fresh_right = jnp.einsum('rc,rk->ck', scaled.astype(jnp.float32), stacked.astype(jnp.float32)) * (1.0 / basis_scale)
        return (scaled.reshape(D, S, S), fresh_right.astype(jnp.bfloat16).reshape(S, D, S))
    scaled_all, right_all = lax.map(one_middle, jnp.arange(SECTORS, dtype=jnp.int32))
    columns_out = []
    for photon in range(D):
        shifted = jnp.concatenate([scaled_all[photon:, photon], jnp.zeros((photon, S, S), jnp.bfloat16)], axis=0)
        columns_out.append(shifted)
    fresh_left = jnp.stack(columns_out, axis=2)
    return (fresh_left, right_all)

def one_bond(inputs):
    left_pair, right_pair, gate_pair, sketch_pair, kept_pair = inputs
    return bond_update(left_pair, right_pair, gate_pair, sketch_pair, kept_pair)

def reference(left_sites, right_sites, pair_gates, test_matrix, kept_columns):
    fresh_lefts, fresh_rights = lax.map(one_bond, (left_sites[:-1], right_sites[1:], pair_gates[:-1], test_matrix[:-1], kept_columns[:-1]))
    new_left = jnp.concatenate([fresh_lefts, left_sites[-1:]], axis=0)
    new_right = jnp.concatenate([right_sites[:1], fresh_rights], axis=0)
    return (new_left, new_right)
```

```python
import functools
import math

import jax
import jax.numpy as jnp
from jax import lax
from jax.experimental import pallas as pl
from jax.experimental.pallas import tpu as pltpu
from jax.sharding import PartitionSpec as P

RIDGE_SHARE = 0.05
TINY_SHIFT = 1e-05
MESH = pl.DeviceIdType.MESH
HIGHEST = lax.Precision.HIGHEST
VMEM_LIMIT = 48 * 1024 * 1024


def ring(index, by, size):
    return lax.rem(index + (by + size), size)


def greet(partners):
    barrier = pltpu.get_barrier_semaphore()
    for partner in partners:
        pl.semaphore_signal(barrier, inc=1, device_id=partner, device_id_type=MESH)
    pl.semaphore_wait(barrier, len(partners))


def gather_kernel(
    levels, chains, sectors,
    gate_ref, left_ref, right_ref, block_ref,
    left_in, right_in,
    chain_send, chain_recv, left_send, left_recv, up_send, up_recv, down_send, down_recv,
):
    chain, sector = lax.axis_index("chain"), lax.axis_index("sector")
    above = (chain, ring(sector, 1, sectors))
    below = (chain, ring(sector, -1, sectors))
    before = (ring(chain, -1, chains), sector)
    after = (ring(chain, 1, chains), sector)
    greet((above, below, before, after))
    last = levels - 1
    size = left_ref.shape[1]

    def slot(offset, r):
        return right_in.at[r + offset, last - r]

    def chain_copy(r):
        return pltpu.make_async_remote_copy(
            src_ref=right_ref.at[r], dst_ref=slot(0, r), send_sem=chain_send.at[r], recv_sem=chain_recv.at[r],
            device_id=before, device_id_type=MESH,
        )

    def left_copy(hop, n):
        source = left_ref.at[n] if hop == 1 else left_in.at[hop - 2, n]
        return pltpu.make_async_remote_copy(
            src_ref=source, dst_ref=left_in.at[hop - 1, n], send_sem=left_send.at[hop - 1, n],
            recv_sem=left_recv.at[hop - 1, n], device_id=above, device_id_type=MESH,
        )

    def up_copy(hop, r):
        return pltpu.make_async_remote_copy(
            src_ref=slot(1 - hop, r), dst_ref=slot(-hop, r), send_sem=up_send.at[hop - 1, r],
            recv_sem=up_recv.at[hop - 1, r], device_id=above, device_id_type=MESH,
        )

    def down_copy(hop, r):
        return pltpu.make_async_remote_copy(
            src_ref=slot(hop - 1, r), dst_ref=slot(hop, r), send_sem=down_send.at[hop - 1, r],
            recv_sem=down_recv.at[hop - 1, r], device_id=below, device_id_type=MESH,
        )

    def build_row(p):
        source = left_ref if p == 0 else left_in.at[p - 1]
        for q in range(levels):
            value = None
            for n in range(levels):
                r = p + q - n
                if 0 <= r <= last:
                    product = jnp.dot(source[n], right_in[q, last - r], preferred_element_type=jnp.float32)
                    product = product.astype(jnp.bfloat16).astype(jnp.float32)
                    term = product * gate_ref[(p * levels + q) * levels + n]
                    value = term if value is None else value + term
            block_ref[p * size:(p + 1) * size, q * size:(q + 1) * size] = value.astype(jnp.bfloat16)

    for r in range(levels):
        chain_copy(r).start()
    for n in range(levels):
        left_copy(1, n).start()
    for r in range(levels):
        chain_copy(r).wait_recv()
        if r < last:
            down_copy(1, r).start()
        if r > 0:
            up_copy(1, r).start()
    for hop in range(1, levels):
        for r in range(levels):
            if r + hop <= last:
                down_copy(hop, r).wait_recv()
                if r + hop < last:
                    down_copy(hop + 1, r).start()
            if r >= hop:
                up_copy(hop, r).wait_recv()
                if r > hop:
                    up_copy(hop + 1, r).start()
        for n in range(levels):
            left_copy(hop, n).wait_recv()
            if hop < last:
                left_copy(hop + 1, n).start()
        for p in range(levels):
            if max(p, last - p) == hop:
                build_row(p)
    for r in range(levels):
        chain_copy(r).wait_send()
    for hop in range(1, levels):
        for r in range(levels):
            left_copy(hop, r).wait_send()
            if r + hop <= last:
                down_copy(hop, r).wait_send()
            if r >= hop:
                up_copy(hop, r).wait_send()


def gather_blocks(gates, left, right, chains, sectors):
    levels, size = left.shape[0], left.shape[1]
    hops = pltpu.SemaphoreType.DMA((levels - 1, levels))
    one = pltpu.SemaphoreType.DMA((levels,))
    return pl.pallas_call(
        functools.partial(gather_kernel, levels, chains, sectors),
        out_shape=jax.ShapeDtypeStruct((levels * size, levels * size), jnp.bfloat16),
        in_specs=[
            pl.BlockSpec(memory_space=pltpu.SMEM),
            pl.BlockSpec(memory_space=pltpu.VMEM),
            pl.BlockSpec(memory_space=pl.ANY),
        ],
        out_specs=pl.BlockSpec(memory_space=pltpu.VMEM),
        scratch_shapes=[
            pltpu.VMEM((levels - 1, levels, size, size), jnp.bfloat16),
            pltpu.VMEM((levels, levels, size, size), jnp.bfloat16),
            one, one, hops, hops, hops, hops, hops, hops,
        ],
        compiler_params=pltpu.CompilerParams(
            collective_id=0, has_side_effects=True, vmem_limit_bytes=VMEM_LIMIT
        ),
    )(gates, left, right)


def scatter_kernel(
    levels, chains, sectors,
    pieces_ref, right_ref, left_out, right_out,
    own_sem, chain_send, chain_recv, send, recv,
):
    chain, sector = lax.axis_index("chain"), lax.axis_index("sector")
    before = (ring(chain, -1, chains), sector)
    after = (ring(chain, 1, chains), sector)
    below = [(chain, ring(sector, -p, sectors)) for p in range(1, levels)]
    above = [(chain, ring(sector, p, sectors)) for p in range(1, levels)]
    greet((before, after, *below, *above))
    own = pltpu.make_async_copy(pieces_ref.at[0], left_out.at[0], own_sem)
    chain_copy = pltpu.make_async_remote_copy(
        src_ref=right_ref, dst_ref=right_out, send_sem=chain_send, recv_sem=chain_recv,
        device_id=after, device_id_type=MESH,
    )
    copies = [
        pltpu.make_async_remote_copy(
            src_ref=pieces_ref.at[p], dst_ref=left_out.at[p], send_sem=send.at[p - 1], recv_sem=recv.at[p - 1],
            device_id=below[p - 1], device_id_type=MESH,
        )
        for p in range(1, levels)
    ]
    for copy in reversed(copies):
        copy.start()
    chain_copy.start()
    own.start()
    own.wait()
    for copy in copies:
        copy.wait()
    chain_copy.wait()


def scatter(pieces, fresh_right, chains, sectors):
    levels = pieces.shape[0]
    return pl.pallas_call(
        functools.partial(scatter_kernel, levels, chains, sectors),
        out_shape=(
            jax.ShapeDtypeStruct(pieces.shape, pieces.dtype),
            jax.ShapeDtypeStruct(fresh_right.shape, fresh_right.dtype),
        ),
        in_specs=[pl.BlockSpec(memory_space=pl.ANY)] * 2,
        out_specs=(pl.BlockSpec(memory_space=pl.ANY),) * 2,
        scratch_shapes=[
            pltpu.SemaphoreType.DMA,
            pltpu.SemaphoreType.DMA,
            pltpu.SemaphoreType.DMA,
            pltpu.SemaphoreType.DMA((levels - 1,)),
            pltpu.SemaphoreType.DMA((levels - 1,)),
        ],
        compiler_params=pltpu.CompilerParams(collective_id=1, has_side_effects=True),
    )(pieces, fresh_right)


def sketch_kernel(block_ref, test_ref, sketch_ref, gram_ref):
    contract_rows = (((0,), (0,)), ((), ()))
    contract_columns = (((1,), (1,)), ((), ()))
    block = block_ref[...]
    first = jnp.dot(block, test_ref[...], preferred_element_type=jnp.float32).astype(jnp.bfloat16)
    back = lax.dot_general(first, block, contract_rows, preferred_element_type=jnp.float32).astype(jnp.bfloat16)
    sketch = lax.dot_general(block, back, contract_columns, preferred_element_type=jnp.float32)
    sketch_ref[...] = sketch
    size = sketch.shape[1]
    gram = lax.dot_general(sketch, sketch, contract_rows, precision=HIGHEST, preferred_element_type=jnp.float32)
    diagonal = lax.broadcasted_iota(jnp.int32, (size, size), 0) == lax.broadcasted_iota(jnp.int32, (size, size), 1)
    trace = jnp.sum(jnp.where(diagonal, gram, 0.0))
    gram_ref[...] = gram + jnp.where(diagonal, RIDGE_SHARE * trace / size + TINY_SHIFT, 0.0)


def make_sketch(block, test_matrix):
    rows, size = test_matrix.shape
    return pl.pallas_call(
        sketch_kernel,
        out_shape=(
            jax.ShapeDtypeStruct((rows, size), jnp.float32),
            jax.ShapeDtypeStruct((size, size), jnp.float32),
        ),
        in_specs=[pl.BlockSpec(memory_space=pltpu.VMEM)] * 2,
        out_specs=(pl.BlockSpec(memory_space=pltpu.VMEM),) * 2,
        compiler_params=pltpu.CompilerParams(vmem_limit_bytes=VMEM_LIMIT),
    )(block, test_matrix)


def inverse_factor_kernel(width, gram_ref, inverse_ref, work):
    size = gram_ref.shape[0]
    contract_rows = (((0,), (0,)), ((), ()))

    def iota(shape, dim):
        return lax.broadcasted_iota(jnp.int32, shape, dim)

    work[:, :size] = gram_ref[...]
    work[:, size:] = jnp.where(iota((size, size), 0) == iota((size, size), 1), 1.0, 0.0)
    for start in range(0, size, width):
        stop = start + width
        eye = jnp.where(iota((width, width), 0) == iota((width, width), 1), 1.0, 0.0)
        local = jnp.concatenate([work[start:stop, start:stop], eye], axis=1)
        rows = [local[8 * t:8 * (t + 1)] for t in range(width // 8)]
        index = iota((8, 2 * width), 0)
        for k in range(0, width, 2):
            t0, s = k // 8, k % 8
            tile = rows[t0]
            row0 = tile[s:s + 1]
            row1 = tile[s + 1:s + 2]
            a = row0[:, k:k + 1]
            b = row0[:, k + 1:k + 2]
            c = row1[:, k + 1:k + 2]
            inv_a = 1.0 / a
            ratio = b * inv_a
            inv_c = 1.0 / (c - b * ratio)
            row1 = row1 - ratio * row0
            scaled0 = row0 * inv_a
            scaled1 = row1 * inv_c
            for t in range(t0, width // 8):
                m0 = rows[t][:, k:k + 1]
                m1 = rows[t][:, k + 1:k + 2] - m0 * ratio
                updated = rows[t] - m0 * scaled0 - m1 * scaled1
                if t == t0:
                    keep = jnp.where(index == s + 1, row1, rows[t])
                    updated = jnp.where(index > s + 1, updated, keep)
                rows[t] = updated
        reduced = jnp.concatenate(rows, axis=0)
        pivots = jnp.sum(reduced[:, :width] * eye, axis=1, keepdims=True)
        small = reduced[:, width:] * lax.rsqrt(pivots)
        top = jnp.dot(small, work[start:stop, :], precision=HIGHEST, preferred_element_type=jnp.float32)
        inverse_ref[start:stop, :] = top[:, size:]
        if stop < size:
            work[stop:, :] -= lax.dot_general(
                top[:, stop:size], top, contract_rows, precision=HIGHEST, preferred_element_type=jnp.float32
            )


def inverse_factor(gram):
    size = gram.shape[0]
    return pl.pallas_call(
        functools.partial(inverse_factor_kernel, min(64, size)),
        out_shape=jax.ShapeDtypeStruct((size, size), jnp.float32),
        in_specs=[pl.BlockSpec(memory_space=pltpu.VMEM)],
        out_specs=pl.BlockSpec(memory_space=pltpu.VMEM),
        scratch_shapes=[pltpu.VMEM((size, 2 * size), jnp.float32)],
        compiler_params=pltpu.CompilerParams(vmem_limit_bytes=VMEM_LIMIT),
    )(gram)


def basis_kernel(scale, kept_ref, block_ref, sketch_ref, inverse_ref, pieces_ref, right_ref):
    contract_rows = (((0,), (0,)), ((), ()))
    contract_columns = (((1,), (1,)), ((), ()))
    basis = lax.dot_general(
        sketch_ref[...], inverse_ref[...], contract_columns, precision=HIGHEST, preferred_element_type=jnp.float32
    )
    column = lax.broadcasted_iota(jnp.int32, basis.shape, 1)
    scaled = (jnp.where(column < kept_ref[0], basis, 0.0) * scale).astype(jnp.bfloat16)
    pieces_ref[...] = scaled
    fresh = lax.dot_general(scaled, block_ref[...], contract_rows, preferred_element_type=jnp.float32)
    fresh = fresh * (1.0 / scale)
    levels, size = right_ref.shape[0], right_ref.shape[1]
    for q in range(levels):
        right_ref[q] = fresh[:, q * size:(q + 1) * size].astype(jnp.bfloat16)


def make_basis(kept, block, sketch, inverse, levels):
    rows, size = sketch.shape
    return pl.pallas_call(
        functools.partial(basis_kernel, math.sqrt(rows)),
        out_shape=(
            jax.ShapeDtypeStruct((rows, size), jnp.bfloat16),
            jax.ShapeDtypeStruct((levels, size, size), jnp.bfloat16),
        ),
        in_specs=[pl.BlockSpec(memory_space=pltpu.SMEM)] + [pl.BlockSpec(memory_space=pltpu.VMEM)] * 3,
        out_specs=(pl.BlockSpec(memory_space=pltpu.VMEM),) * 2,
        compiler_params=pltpu.CompilerParams(vmem_limit_bytes=VMEM_LIMIT),
    )(kept, block, sketch, inverse)


def level_gates(gates, levels, sector, sectors):
    p = jnp.arange(levels)[:, None, None]
    q = jnp.arange(levels)[None, :, None]
    n = jnp.arange(levels)[None, None, :]
    r = p + q - n
    inside = (r >= 0) & (r < levels)
    r = jnp.clip(r, 0, levels - 1)
    chosen = gates.astype(jnp.float32)[p * levels + q, n * levels + r]
    inside = inside & (sector - p >= 0) & (sector + q < sectors)
    return jnp.where(inside, chosen, 0.0).reshape(-1)


def per_device(left_sites, right_sites, pair_gates, test_matrix, kept_columns):
    levels = left_sites.shape[3]
    size = left_sites.shape[2]
    sectors = lax.axis_size("sector")
    sector = lax.axis_index("sector")
    chains = lax.axis_size("chain")
    chain = lax.axis_index("chain")
    left = jnp.transpose(left_sites[0, 0], (1, 0, 2))
    right = jnp.transpose(right_sites[0, 0], (1, 0, 2))
    gates = level_gates(pair_gates[0], levels, sector, sectors)
    block = gather_blocks(gates, left, right, chains, sectors)
    sketch, gram = make_sketch(block, test_matrix[0, 0])
    inverse = inverse_factor(gram)
    pieces, fresh_right = make_basis(kept_columns[0], block, sketch, inverse, levels)
    fresh_left, shipped = scatter(pieces.reshape(levels, size, size), fresh_right, chains, sectors)
    inside = sector + jnp.arange(levels)[:, None, None] < sectors
    fresh_left = jnp.where(inside, fresh_left, jnp.zeros_like(fresh_left))
    new_left = jnp.where(chain == chains - 1, left, fresh_left)
    new_right = jnp.where(chain == 0, right, shipped)
    return (
        jnp.transpose(new_left, (1, 0, 2))[None, None],
        jnp.transpose(new_right, (1, 0, 2))[None, None],
    )


def solution(mesh):
    return jax.shard_map(
        per_device,
        mesh=mesh,
        in_specs=(
            P("chain", "sector", None, None, None),
            P("chain", "sector", None, None, None),
            P("chain", None, None),
            P("chain", "sector", None, None),
            P("chain", "sector"),
        ),
        out_specs=(P("chain", "sector", None, None, None), P("chain", "sector", None, None, None)),
        check_vma=False,
    )
```

```python
import functools
import math

import jax
import jax.numpy as jnp
from jax import lax
from jax.experimental import pallas as pl
from jax.experimental.pallas import tpu as pltpu
from jax.sharding import PartitionSpec as P

RIDGE_SHARE = 0.05
TINY_SHIFT = 1e-05
MESH = pl.DeviceIdType.MESH
HIGHEST = lax.Precision.HIGHEST
VMEM_LIMIT = 56 * 1024 * 1024
ROWS = (((0,), (0,)), ((), ()))
COLUMNS = (((1,), (1,)), ((), ()))


def ring(index, by, size):
    return lax.rem(index + (by + size), size)


def iota(shape, dim):
    return lax.broadcasted_iota(jnp.int32, shape, dim)


def identity(size):
    return jnp.where(iota((size, size), 0) == iota((size, size), 1), 1.0, 0.0)


def eliminate(local, width):
    shape = (8, 2 * width)
    tiles = [local[8 * t:8 * (t + 1)] for t in range(width // 8)]
    index = iota(shape, 0)
    for t0 in range(width // 8):
        columns = [
            [jnp.broadcast_to(tile[:, 8 * t0 + j:8 * t0 + j + 1], shape) for tile in tiles[t0:]] for j in range(8)
        ]
        rows = [jnp.broadcast_to(tiles[t0][j:j + 1], shape) for j in range(8)]
        pivots = [[jnp.broadcast_to(columns[l][0][j:j + 1], shape) for l in range(j + 1)] for j in range(8)]
        scaled = []
        for j in range(8):
            inverse = 1.0 / pivots[j][j]
            for i in range(j + 1, 8):
                share = pivots[i][j] * inverse
                for l in range(j + 1, i + 1):
                    pivots[i][l] = pivots[i][l] - share * pivots[l][j]
                rows[i] = rows[i] - share * rows[j]
                columns[i] = [x - share * y for x, y in zip(columns[i], columns[j])]
            scaled.append(rows[j] * inverse)
        kept = tiles[t0]
        for j in range(1, 8):
            kept = jnp.where(index == j, rows[j], kept)
        tiles[t0] = kept
        for t in range(t0 + 1, width // 8):
            for j in range(8):
                tiles[t] = tiles[t] - columns[j][t - t0] * scaled[j]
    return jnp.concatenate(tiles, axis=0)


def invert_factor(width, work):
    size = work.shape[0]
    for start in range(0, size, width):
        stop = start + width
        eye = identity(width)
        reduced = eliminate(jnp.concatenate([work[start:stop, start:stop], eye], axis=1), width)
        pivots = jnp.sum(reduced[:, :width] * eye, axis=1, keepdims=True)
        small = reduced[:, width:] * lax.rsqrt(pivots)
        top = jnp.dot(small, work[start:stop, :], precision=HIGHEST, preferred_element_type=jnp.float32)
        work[start:stop, size:] = top[:, size:]
        if stop < size:
            work[stop:, :] -= lax.dot_general(
                top[:, stop:size], top, ROWS, precision=HIGHEST, preferred_element_type=jnp.float32
            )


def layer_kernel(
    levels, chains, sectors,
    gate_ref, kept_ref, left_ref, test_ref, right_ref,
    left_out, right_out,
    left_in, right_in, total, block, back_total, sketch, work, pieces, fresh,
    chain_send, chain_recv, left_send, left_recv, far_send, far_recv, up_send, up_recv, down_send, down_recv,
    piece_send, piece_recv, fresh_send, fresh_recv, own_sem,
):
    chain, sector = lax.axis_index("chain"), lax.axis_index("sector")
    above = [(chain, ring(sector, p, sectors)) for p in range(levels)]
    below = [(chain, ring(sector, -p, sectors)) for p in range(levels)]
    before = (ring(chain, -1, chains), sector)
    after = (ring(chain, 1, chains), sector)
    partners = (before, after, *above[1:], *below[1:])
    last = levels - 1
    size = left_ref.shape[1]
    near = last - 2
    turned = levels // 2

    def remote(source, target, send_sem, recv_sem, device):
        return pltpu.make_async_remote_copy(
            src_ref=source, dst_ref=target, send_sem=send_sem, recv_sem=recv_sem, device_id=device, device_id_type=MESH
        )

    def slot(offset, r):
        return right_in.at[r + offset, last - r]

    def chain_copy(r):
        return remote(right_ref.at[r], slot(0, r), chain_send.at[r], chain_recv.at[r], before)

    def left_copy(hop, n):
        sems = left_send.at[hop - 1, n], left_recv.at[hop - 1, n]
        if hop == near + 1 and n < turned:
            return remote(left_in.at[last - 1, n], left_in.at[hop - 1, n], *sems, below[1])
        source = left_ref.at[n] if hop == 1 else left_in.at[hop - 2, n]
        return remote(source, left_in.at[hop - 1, n], *sems, above[1])

    def far_copy(n):
        return remote(left_ref.at[n], left_in.at[last - 1, n], far_send.at[n], far_recv.at[n], above[last])

    def up_copy(hop, r):
        return remote(slot(1 - hop, r), slot(-hop, r), up_send.at[hop - 1, r], up_recv.at[hop - 1, r], above[1])

    def down_copy(hop, r):
        return remote(slot(hop - 1, r), slot(hop, r), down_send.at[hop - 1, r], down_recv.at[hop - 1, r], below[1])

    def piece_copy(p):
        return remote(pieces.at[p], left_out.at[p], piece_send.at[p - 1], piece_recv.at[p - 1], below[p])

    def fresh_copy(q):
        return remote(fresh.at[q], right_out.at[q], fresh_send.at[q], fresh_recv.at[q], after)

    def gate(p, q, n):
        inside = (sector >= p) & (sector + q < sectors)
        return jnp.where(inside, gate_ref[p * levels + q, n * levels + p + q - n], 0.0)

    def add_term(p, n):
        source = left_ref.at[n] if p == 0 else left_in.at[p - 1, n]
        for q in range(levels):
            r = p + q - n
            if 0 <= r <= last:
                product = jnp.dot(source[...], right_in[q, last - r], preferred_element_type=jnp.float32)
                term = product.astype(jnp.bfloat16).astype(jnp.float32) * gate(p, q, n)
                if n == max(0, p + q - last):
                    total[p, q] = term
                else:
                    total[p, q] += term

    def finish_row(p):
        for q in range(levels):
            block[p * size:(p + 1) * size, q * size:(q + 1) * size] = total[p, q].astype(jnp.bfloat16)
        row = block[p * size:(p + 1) * size, :]
        first = jnp.dot(row, test_ref[...], preferred_element_type=jnp.float32).astype(jnp.bfloat16)
        back_total[...] += lax.dot_general(first, row, ROWS, preferred_element_type=jnp.float32)

    barrier = pltpu.get_barrier_semaphore()
    for partner in partners:
        pl.semaphore_signal(barrier, inc=1, device_id=partner, device_id_type=MESH)
    pl.semaphore_wait(barrier, len(partners))

    queue = []

    def ready(hop):
        for p in range(min(hop, near) + 1):
            for n in range(levels):
                if max(p, abs(n - p)) == hop:
                    queue.append(functools.partial(add_term, p, n))
                    if n == last:
                        queue.append(functools.partial(finish_row, p))

    def work_on(count):
        for _ in range(min(count, len(queue))):
            queue.pop(0)()

    for r in range(levels):
        chain_copy(r).start()
    for n in range(levels):
        left_copy(1, n).start()
    for n in range(levels):
        far_copy(n).start()
    back_total[...] = jnp.zeros_like(back_total)
    for r in range(levels):
        chain_copy(r).wait_recv()
        if r < last:
            down_copy(1, r).start()
        if r > 0:
            up_copy(1, r).start()
    ready(0)
    for hop in range(1, levels):
        for n in range(levels):
            if hop <= near:
                left_copy(hop, n).wait_recv()
                if hop < near or n >= turned:
                    left_copy(hop + 1, n).start()
            if n >= hop:
                up_copy(hop, n).wait_recv()
                if n > hop:
                    up_copy(hop + 1, n).start()
            if n + hop <= last:
                down_copy(hop, n).wait_recv()
                if n + hop < last:
                    down_copy(hop + 1, n).start()
            work_on(2)
        if hop == 2:
            for n in range(turned):
                far_copy(n).wait_recv()
                left_copy(near + 1, n).start()
        ready(hop)
    work_on(len(queue))
    for p in range(near + 1, levels):
        for n in range(levels):
            if p < last:
                left_copy(p, n).wait_recv()
            elif n >= turned:
                far_copy(n).wait_recv()
            add_term(p, n)
        finish_row(p)

    back = back_total[...].astype(jnp.bfloat16)
    sketch[...] = lax.dot_general(block[...], back, COLUMNS, preferred_element_type=jnp.float32)
    gram = lax.dot_general(sketch[...], sketch[...], ROWS, precision=HIGHEST, preferred_element_type=jnp.float32)
    eye = identity(size)
    ridge = RIDGE_SHARE * jnp.sum(gram * eye) / size + TINY_SHIFT
    work[:, :size] = gram + ridge * eye
    work[:, size:] = eye
    invert_factor(min(64, size), work)
    basis = lax.dot_general(sketch[...], work[:, size:], COLUMNS, precision=HIGHEST, preferred_element_type=jnp.float32)
    scale = math.sqrt(levels * size)
    scaled = jnp.where(iota(basis.shape, 1) < kept_ref[0, 0], basis, 0.0) * scale
    scaled = scaled.astype(jnp.bfloat16)
    for p in range(levels):
        pieces[p] = scaled[p * size:(p + 1) * size]
    for p in range(last, 0, -1):
        piece_copy(p).start()
    own_copy = pltpu.make_async_copy(pieces.at[0], left_out.at[0], own_sem)
    own_copy.start()
    new_right = lax.dot_general(scaled, block[...], ROWS, preferred_element_type=jnp.float32) * (1.0 / scale)
    for q in range(levels):
        fresh[q] = new_right[:, q * size:(q + 1) * size].astype(jnp.bfloat16)
        fresh_copy(q).start()
    for r in range(levels):
        chain_copy(r).wait_send()
        far_copy(r).wait_send()
    for hop in range(1, levels):
        for r in range(levels):
            if hop < last:
                left_copy(hop, r).wait_send()
            if r + hop <= last:
                down_copy(hop, r).wait_send()
            if r >= hop:
                up_copy(hop, r).wait_send()
    own_copy.wait()
    for q in range(levels):
        fresh_copy(q).wait()
    for p in range(1, levels):
        piece_copy(p).wait()


def run_layer(gates, kept, left, right, test_matrix, chains, sectors):
    levels, size = left.shape[0], left.shape[1]
    hops = pltpu.SemaphoreType.DMA((levels - 1, levels))
    one = pltpu.SemaphoreType.DMA((levels,))
    part = (levels, size, size)
    return pl.pallas_call(
        functools.partial(layer_kernel, levels, chains, sectors),
        out_shape=(jax.ShapeDtypeStruct(part, jnp.bfloat16), jax.ShapeDtypeStruct(part, jnp.bfloat16)),
        in_specs=[
            pl.BlockSpec(memory_space=pltpu.SMEM),
            pl.BlockSpec(memory_space=pltpu.SMEM),
            pl.BlockSpec(memory_space=pltpu.VMEM),
            pl.BlockSpec(memory_space=pltpu.VMEM),
            pl.BlockSpec(memory_space=pl.ANY),
        ],
        out_specs=(pl.BlockSpec(memory_space=pl.ANY),) * 2,
        scratch_shapes=[
            pltpu.VMEM((levels - 1, *part), jnp.bfloat16),
            pltpu.VMEM((levels, *part), jnp.bfloat16),
            pltpu.VMEM((levels, *part), jnp.float32),
            pltpu.VMEM((levels * size, levels * size), jnp.bfloat16),
            pltpu.VMEM((size, levels * size), jnp.float32),
            pltpu.VMEM((levels * size, size), jnp.float32),
            pltpu.VMEM((size, 2 * size), jnp.float32),
            pltpu.VMEM(part, jnp.bfloat16),
            pltpu.VMEM(part, jnp.bfloat16),
            one, one, hops, hops, one, one, hops, hops, hops, hops, one, one, one, one,
            pltpu.SemaphoreType.DMA,
        ],
        compiler_params=pltpu.CompilerParams(
            collective_id=0, has_side_effects=True, vmem_limit_bytes=VMEM_LIMIT
        ),
    )(gates, kept, left, test_matrix, right)


def per_device(left_sites, right_sites, pair_gates, test_matrix, kept_columns):
    levels = left_sites.shape[3]
    sectors = lax.axis_size("sector")
    sector = lax.axis_index("sector")
    chains = lax.axis_size("chain")
    chain = lax.axis_index("chain")
    left = jnp.transpose(left_sites[0, 0], (1, 0, 2))
    right = jnp.transpose(right_sites[0, 0], (1, 0, 2))
    gates = pair_gates[0].astype(jnp.float32)
    fresh_left, shipped = run_layer(gates, kept_columns, left, right, test_matrix[0, 0], chains, sectors)
    inside = sector + jnp.arange(levels)[:, None, None] < sectors
    fresh_left = jnp.where(inside, fresh_left, jnp.zeros_like(fresh_left))
    new_left = jnp.where(chain == chains - 1, left, fresh_left)
    new_right = jnp.where(chain == 0, right, shipped)
    return (
        jnp.transpose(new_left, (1, 0, 2))[None, None],
        jnp.transpose(new_right, (1, 0, 2))[None, None],
    )


def solution(mesh):
    return jax.shard_map(
        per_device,
        mesh=mesh,
        in_specs=(
            P("chain", "sector", None, None, None),
            P("chain", "sector", None, None, None),
            P("chain", None, None),
            P("chain", "sector", None, None),
            P("chain", "sector"),
        ),
        out_specs=(P("chain", "sector", None, None, None), P("chain", "sector", None, None, None)),
        check_vma=False,
    )
```

```python
import functools
import math

import jax
import jax.numpy as jnp
from jax import lax
from jax.experimental import pallas as pl
from jax.experimental.pallas import tpu as pltpu
from jax.sharding import PartitionSpec as P

RIDGE_SHARE = 0.05
TINY_SHIFT = 1e-05
MESH = pl.DeviceIdType.MESH
HIGHEST = lax.Precision.HIGHEST
VMEM_LIMIT = 56 * 1024 * 1024
ROWS = (((0,), (0,)), ((), ()))
COLUMNS = (((1,), (1,)), ((), ()))


def ring(index, by, size):
    return lax.rem(index + (by + size), size)


def iota(shape, dim):
    return lax.broadcasted_iota(jnp.int32, shape, dim)


def identity(size):
    return jnp.where(iota((size, size), 0) == iota((size, size), 1), 1.0, 0.0)


def eliminate(local, width):
    shape = (8, 2 * width)
    tiles = [local[8 * t:8 * (t + 1)] for t in range(width // 8)]
    index = iota(shape, 0)
    for t0 in range(width // 8):
        columns = [
            [jnp.broadcast_to(tile[:, 8 * t0 + j:8 * t0 + j + 1], shape) for tile in tiles[t0:]] for j in range(8)
        ]
        rows = [jnp.broadcast_to(tiles[t0][j:j + 1], shape) for j in range(8)]
        pivots = [[jnp.broadcast_to(columns[l][0][j:j + 1], shape) for l in range(j + 1)] for j in range(8)]
        scaled = []
        for j in range(8):
            inverse = 1.0 / pivots[j][j]
            for i in range(j + 1, 8):
                share = pivots[i][j] * inverse
                for l in range(j + 1, i + 1):
                    pivots[i][l] = pivots[i][l] - share * pivots[l][j]
                rows[i] = rows[i] - share * rows[j]
                columns[i] = [x - share * y for x, y in zip(columns[i], columns[j])]
            scaled.append(rows[j] * inverse)
        kept = tiles[t0]
        for j in range(1, 8):
            kept = jnp.where(index == j, rows[j], kept)
        tiles[t0] = kept
        for t in range(t0 + 1, width // 8):
            for j in range(8):
                tiles[t] = tiles[t] - columns[j][t - t0] * scaled[j]
    return jnp.concatenate(tiles, axis=0)


def invert_factor(width, work, begin, end):
    size = work.shape[0]
    for start in range(begin, end, width):
        stop = start + width
        eye = identity(width)
        reduced = eliminate(jnp.concatenate([work[start:stop, start:stop], eye], axis=1), width)
        pivots = jnp.sum(reduced[:, :width] * eye, axis=1, keepdims=True)
        small = reduced[:, width:] * lax.rsqrt(pivots)
        top = jnp.dot(small, work[start:stop, :], precision=HIGHEST, preferred_element_type=jnp.float32)
        work[start:stop, size:] = top[:, size:]
        if stop < size:
            work[stop:, :] -= lax.dot_general(
                top[:, stop:size], top, ROWS, precision=HIGHEST, preferred_element_type=jnp.float32
            )


def layer_kernel(
    levels, chains, sectors,
    gate_ref, kept_ref, left_ref, test_ref, right_ref,
    left_out, right_out,
    left_in, right_in, total, block, back_total, sketch, work, pieces, fresh,
    chain_send, chain_recv, left_send, left_recv, far_send, far_recv, up_send, up_recv, down_send, down_recv,
    piece_send, piece_recv, fresh_send, fresh_recv, own_sem,
):
    chain, sector = lax.axis_index("chain"), lax.axis_index("sector")
    above = [(chain, ring(sector, p, sectors)) for p in range(levels)]
    below = [(chain, ring(sector, -p, sectors)) for p in range(levels)]
    before = (ring(chain, -1, chains), sector)
    after = (ring(chain, 1, chains), sector)
    partners = (before, after, *above[1:], *below[1:])
    last = levels - 1
    size = left_ref.shape[1]
    near = last - 2
    turned = levels // 2

    def remote(source, target, send_sem, recv_sem, device):
        return pltpu.make_async_remote_copy(
            src_ref=source, dst_ref=target, send_sem=send_sem, recv_sem=recv_sem, device_id=device, device_id_type=MESH
        )

    def slot(offset, r):
        return right_in.at[r + offset, last - r]

    def chain_copy(r):
        return remote(right_ref.at[r], slot(0, r), chain_send.at[r], chain_recv.at[r], before)

    def left_copy(hop, n):
        sems = left_send.at[hop - 1, n], left_recv.at[hop - 1, n]
        if hop == near + 1 and n < turned:
            return remote(left_in.at[last - 1, n], left_in.at[hop - 1, n], *sems, below[1])
        source = left_ref.at[n] if hop == 1 else left_in.at[hop - 2, n]
        return remote(source, left_in.at[hop - 1, n], *sems, above[1])

    def far_copy(n):
        return remote(left_ref.at[n], left_in.at[last - 1, n], far_send.at[n], far_recv.at[n], above[last])

    def up_copy(hop, r):
        return remote(slot(1 - hop, r), slot(-hop, r), up_send.at[hop - 1, r], up_recv.at[hop - 1, r], above[1])

    def down_copy(hop, r):
        return remote(slot(hop - 1, r), slot(hop, r), down_send.at[hop - 1, r], down_recv.at[hop - 1, r], below[1])

    def columns(part):
        return pl.ds(part * (size // 2), size // 2)

    def piece_copy(part, p):
        target = left_out.at[p, :, columns(part)]
        return remote(pieces.at[part, p], target, piece_send.at[part, p - 1], piece_recv.at[part, p - 1], below[p])

    def own_copy(part):
        return pltpu.make_async_copy(pieces.at[part, 0], left_out.at[0, :, columns(part)], own_sem.at[part])

    def fresh_copy(q):
        return remote(fresh.at[q], right_out.at[q], fresh_send.at[q], fresh_recv.at[q], after)

    def gate(p, q, n):
        inside = (sector >= p) & (sector + q < sectors)
        return jnp.where(inside, gate_ref[p * levels + q, n * levels + p + q - n], 0.0)

    def add_term(p, n):
        source = left_ref.at[n] if p == 0 else left_in.at[p - 1, n]
        for q in range(levels):
            r = p + q - n
            if 0 <= r <= last:
                product = jnp.dot(source[...], right_in[q, last - r], preferred_element_type=jnp.float32)
                term = product.astype(jnp.bfloat16).astype(jnp.float32) * gate(p, q, n)
                if (p, q) in begun:
                    total[p, q] += term
                else:
                    total[p, q] = term
                    begun.add((p, q))

    def finish_row(p):
        for q in range(levels):
            block[p * size:(p + 1) * size, q * size:(q + 1) * size] = total[p, q].astype(jnp.bfloat16)
        row = block[p * size:(p + 1) * size, :]
        first = jnp.dot(row, test_ref[...], preferred_element_type=jnp.float32).astype(jnp.bfloat16)
        back_total[...] += lax.dot_general(first, row, ROWS, preferred_element_type=jnp.float32)

    barrier = pltpu.get_barrier_semaphore()
    for partner in partners:
        pl.semaphore_signal(barrier, inc=1, device_id=partner, device_id_type=MESH)
    pl.semaphore_wait(barrier, len(partners))

    queue, here, queued, begun = [], set(), set(), set()
    terms_left = [levels] * levels

    def needs(p, n):
        offset = n - p
        slices = range(max(0, -offset), min(last, last - offset) + 1)
        return {("left", p, n)} | {("right", offset, r) for r in slices}

    def arrived(*what):
        here.add(what)
        for p in range(levels):
            for n in range(levels):
                if (p, n) not in queued and needs(p, n) <= here:
                    queued.add((p, n))
                    queue.append((p, n))

    def work_on(count):
        for _ in range(min(count, len(queue))):
            p, n = queue.pop(0)
            add_term(p, n)
            terms_left[p] -= 1
            if terms_left[p] == 0:
                finish_row(p)

    order = sorted(range(levels), key=lambda r: -max(r, last - r))
    for r in order:
        chain_copy(r).start()
    for n in range(levels):
        left_copy(1, n).start()
        arrived("left", 0, n)
    for n in range(2):
        far_copy(n).start()
    back_total[...] = jnp.zeros_like(back_total)
    for r in order:
        chain_copy(r).wait_recv()
        if r < last:
            down_copy(1, r).start()
        if r > 0:
            up_copy(1, r).start()
        arrived("right", 0, r)
    for hop in range(1, levels):
        for step in range(levels - hop):
            up, down = last - step, step
            up_copy(hop, up).wait_recv()
            if up > hop:
                up_copy(hop + 1, up).start()
            down_copy(hop, down).wait_recv()
            if down + hop < last:
                down_copy(hop + 1, down).start()
            arrived("right", -hop, up)
            arrived("right", hop, down)
            work_on(1)
        for n in range(levels):
            if hop <= near:
                left_copy(hop, n).wait_recv()
                if hop < near or n >= turned:
                    left_copy(hop + 1, n).start()
                arrived("left", hop, n)
                if n == 0 and 2 * hop < levels:
                    for far in range(2 * hop, min(2 * hop + 2, levels)):
                        far_copy(far).start()
                if hop == near and n < turned:
                    far_copy(n).wait_recv()
                    left_copy(near + 1, n).start()
                    arrived("left", last, n)
            elif hop == near + 1:
                left_copy(hop, n).wait_recv()
                arrived("left", hop, n)
            elif n >= turned:
                far_copy(n).wait_recv()
                arrived("left", hop, n)
            work_on(2)
    work_on(len(queue))

    back = back_total[...].astype(jnp.bfloat16)
    sketch[...] = lax.dot_general(block[...], back, COLUMNS, preferred_element_type=jnp.float32)
    gram = lax.dot_general(sketch[...], sketch[...], ROWS, precision=HIGHEST, preferred_element_type=jnp.float32)
    eye = identity(size)
    ridge = RIDGE_SHARE * jnp.sum(gram * eye) / size + TINY_SHIFT
    work[:, :size] = gram + ridge * eye
    work[:, size:] = eye
    scale = math.sqrt(levels * size)
    half = size // 2
    for part in range(2):
        begin = part * half
        invert_factor(min(64, half), work, begin, begin + half)
        basis = lax.dot_general(
            sketch[:, :begin + half], work[begin:begin + half, size:size + begin + half], COLUMNS,
            precision=HIGHEST, preferred_element_type=jnp.float32,
        )
        scaled = jnp.where(iota(basis.shape, 1) + begin < kept_ref[0, 0], basis, 0.0) * scale
        for p in range(levels):
            pieces[part, p] = scaled[p * size:(p + 1) * size].astype(jnp.bfloat16)
        for p in range(last, 0, -1):
            piece_copy(part, p).start()
        own_copy(part).start()
    for part in range(2):
        scaled = pieces[part].reshape(levels * size, half)
        new_right = lax.dot_general(scaled, block[...], ROWS, preferred_element_type=jnp.float32) * (1.0 / scale)
        for q in range(levels):
            fresh[q, part * half:(part + 1) * half] = new_right[:, q * size:(q + 1) * size].astype(jnp.bfloat16)
    for q in range(levels):
        fresh_copy(q).start()
    for r in range(levels):
        chain_copy(r).wait_send()
        far_copy(r).wait_send()
    for hop in range(1, levels):
        for r in range(levels):
            if hop < last:
                left_copy(hop, r).wait_send()
            if r + hop <= last:
                down_copy(hop, r).wait_send()
            if r >= hop:
                up_copy(hop, r).wait_send()
    for q in range(levels):
        fresh_copy(q).wait()
    for part in range(2):
        own_copy(part).wait()
        for p in range(1, levels):
            piece_copy(part, p).wait()


def run_layer(gates, kept, left, right, test_matrix, chains, sectors):
    levels, size = left.shape[0], left.shape[1]
    hops = pltpu.SemaphoreType.DMA((levels - 1, levels))
    one = pltpu.SemaphoreType.DMA((levels,))
    halves = pltpu.SemaphoreType.DMA((2, levels - 1))
    part = (levels, size, size)
    return pl.pallas_call(
        functools.partial(layer_kernel, levels, chains, sectors),
        out_shape=(jax.ShapeDtypeStruct(part, jnp.bfloat16), jax.ShapeDtypeStruct(part, jnp.bfloat16)),
        in_specs=[
            pl.BlockSpec(memory_space=pltpu.SMEM),
            pl.BlockSpec(memory_space=pltpu.SMEM),
            pl.BlockSpec(memory_space=pltpu.VMEM),
            pl.BlockSpec(memory_space=pltpu.VMEM),
            pl.BlockSpec(memory_space=pl.ANY),
        ],
        out_specs=(pl.BlockSpec(memory_space=pl.ANY),) * 2,
        scratch_shapes=[
            pltpu.VMEM((levels - 1, *part), jnp.bfloat16),
            pltpu.VMEM((levels, *part), jnp.bfloat16),
            pltpu.VMEM((levels, *part), jnp.float32),
            pltpu.VMEM((levels * size, levels * size), jnp.bfloat16),
            pltpu.VMEM((size, levels * size), jnp.float32),
            pltpu.VMEM((levels * size, size), jnp.float32),
            pltpu.VMEM((size, 2 * size), jnp.float32),
            pltpu.VMEM((2, levels, size, size // 2), jnp.bfloat16),
            pltpu.VMEM(part, jnp.bfloat16),
            one, one, hops, hops, one, one, hops, hops, hops, hops, halves, halves, one, one,
            pltpu.SemaphoreType.DMA((2,)),
        ],
        compiler_params=pltpu.CompilerParams(
            collective_id=0, has_side_effects=True, vmem_limit_bytes=VMEM_LIMIT
        ),
    )(gates, kept, left, test_matrix, right)


def per_device(left_sites, right_sites, pair_gates, test_matrix, kept_columns):
    levels = left_sites.shape[3]
    sectors = lax.axis_size("sector")
    sector = lax.axis_index("sector")
    chains = lax.axis_size("chain")
    chain = lax.axis_index("chain")
    left = jnp.transpose(left_sites[0, 0], (1, 0, 2))
    right = jnp.transpose(right_sites[0, 0], (1, 0, 2))
    gates = pair_gates[0].astype(jnp.float32)
    fresh_left, shipped = run_layer(gates, kept_columns, left, right, test_matrix[0, 0], chains, sectors)
    inside = sector + jnp.arange(levels)[:, None, None] < sectors
    fresh_left = jnp.where(inside, fresh_left, jnp.zeros_like(fresh_left))
    new_left = jnp.where(chain == chains - 1, left, fresh_left)
    new_right = jnp.where(chain == 0, right, shipped)
    return (
        jnp.transpose(new_left, (1, 0, 2))[None, None],
        jnp.transpose(new_right, (1, 0, 2))[None, None],
    )


def solution(mesh):
    return jax.shard_map(
        per_device,
        mesh=mesh,
        in_specs=(
            P("chain", "sector", None, None, None),
            P("chain", "sector", None, None, None),
            P("chain", None, None),
            P("chain", "sector", None, None),
            P("chain", "sector"),
        ),
        out_specs=(P("chain", "sector", None, None, None), P("chain", "sector", None, None, None)),
        check_vma=False,
    )
```

```python
import functools
import math

import jax
import jax.numpy as jnp
from jax import lax
from jax.experimental import pallas as pl
from jax.experimental.pallas import tpu as pltpu
from jax.sharding import PartitionSpec as P

RIDGE_SHARE = 0.05
TINY_SHIFT = 1e-05
MESH = pl.DeviceIdType.MESH
HIGHEST = lax.Precision.HIGHEST
VMEM_LIMIT = 56 * 1024 * 1024
ROWS = (((0,), (0,)), ((), ()))
COLUMNS = (((1,), (1,)), ((), ()))


def ring(index, by, size):
    return lax.rem(index + (by + size), size)


def iota(shape, dim):
    return lax.broadcasted_iota(jnp.int32, shape, dim)


def identity(size):
    return jnp.where(iota((size, size), 0) == iota((size, size), 1), 1.0, 0.0)


def eliminate(local, width):
    shape = (8, 2 * width)
    tiles = [local[8 * t:8 * (t + 1)] for t in range(width // 8)]
    index = iota(shape, 0)
    for t0 in range(width // 8):
        columns = [
            [jnp.broadcast_to(tile[:, 8 * t0 + j:8 * t0 + j + 1], shape) for tile in tiles[t0:]] for j in range(8)
        ]
        rows = [jnp.broadcast_to(tiles[t0][j:j + 1], shape) for j in range(8)]
        pivots = [[jnp.broadcast_to(columns[l][0][j:j + 1], shape) for l in range(j + 1)] for j in range(8)]
        scaled = []
        for j in range(8):
            inverse = 1.0 / pivots[j][j]
            for i in range(j + 1, 8):
                share = pivots[i][j] * inverse
                for l in range(j + 1, i + 1):
                    pivots[i][l] = pivots[i][l] - share * pivots[l][j]
                rows[i] = rows[i] - share * rows[j]
                columns[i] = [x - share * y for x, y in zip(columns[i], columns[j])]
            scaled.append(rows[j] * inverse)
        kept = tiles[t0]
        for j in range(1, 8):
            kept = jnp.where(index == j, rows[j], kept)
        tiles[t0] = kept
        for t in range(t0 + 1, width // 8):
            for j in range(8):
                tiles[t] = tiles[t] - columns[j][t - t0] * scaled[j]
    return jnp.concatenate(tiles, axis=0)


def invert_factor(width, work, begin, end):
    size = work.shape[0]
    for start in range(begin, end, width):
        stop = start + width
        eye = identity(width)
        reduced = eliminate(jnp.concatenate([work[start:stop, start:stop], eye], axis=1), width)
        pivots = jnp.sum(reduced[:, :width] * eye, axis=1, keepdims=True)
        small = reduced[:, width:] * lax.rsqrt(pivots)
        top = jnp.dot(small, work[start:stop, begin:], precision=HIGHEST, preferred_element_type=jnp.float32)
        work[start:stop, begin:] = top
        if stop < end:
            work[stop:end, begin:] -= lax.dot_general(
                top[:, stop - begin:end - begin], top, ROWS, precision=HIGHEST, preferred_element_type=jnp.float32
            )


def layer_kernel(
    levels, chains, sectors,
    gate_ref, kept_ref, left_ref, test_ref, right_ref,
    left_out, right_out,
    test_in, kept_in, left_in, right_in, lowest, total, block, back_total, sketch, work, pieces, fresh,
    chain_send, chain_recv, test_send, test_recv, kept_send, kept_recv, left_send, left_recv, up_send, up_recv, down_send, down_recv,
    piece_send, piece_recv, fresh_send, fresh_recv, own_sem,
):
    chain, sector = lax.axis_index("chain"), lax.axis_index("sector")
    above = [(chain, ring(sector, p, sectors)) for p in range(levels)]
    below = [(chain, ring(sector, -p, sectors)) for p in range(levels)]
    before = (ring(chain, -1, chains), sector)
    after = (ring(chain, 1, chains), sector)
    owner = (ring(chain, 1, chains), ring(sector, 1, sectors))
    maker = (ring(chain, -1, chains), ring(sector, -1, sectors))
    partners = (before, after, owner, maker, *above[1:levels - 1], *below[1:levels - 1])
    middle = ring(sector, 1, sectors)
    last = levels - 1
    size = left_ref.shape[1]

    def remote(source, target, send_sem, recv_sem, device):
        return pltpu.make_async_remote_copy(
            src_ref=source, dst_ref=target, send_sem=send_sem, recv_sem=recv_sem, device_id=device, device_id_type=MESH
        )

    def slot(offset, r):
        return right_in.at[r + offset, last - r]

    def place(offset, r):
        return lowest if offset + r < 0 else slot(offset, r)

    def chain_copy(r):
        return remote(right_ref.at[r], place(-1, r), chain_send.at[r], chain_recv.at[r], before)

    def left_at(p, n):
        return left_ref.at[n] if p == 1 else left_in.at[p, n]

    def left_copy(p, n):
        source, device = (left_at(1, n), below[1]) if p == 0 else (left_at(p - 1, n), above[1])
        return remote(source, left_in.at[p, n], left_send.at[p, n], left_recv.at[p, n], device)

    def up_copy(offset, r):
        sems = up_send.at[-offset, r], up_recv.at[-offset, r]
        return remote(slot(offset + 1, r), slot(offset, r), *sems, above[1])

    def down_copy(offset, r):
        sems = down_send.at[offset, r], down_recv.at[offset, r]
        return remote(place(offset - 1, r), slot(offset, r), *sems, below[1])

    def test_copy(n):
        rows = pl.ds(n * size, size)
        return remote(test_ref.at[rows], test_in.at[rows], test_send.at[n], test_recv.at[n], below[1])

    kept_copy = remote(kept_ref, kept_in, kept_send, kept_recv, below[1])

    def columns(part):
        return pl.ds(part * (size // 2), size // 2)

    def piece_copy(part, p):
        target, sems = left_out.at[p, :, columns(part)], (piece_send.at[part, p], piece_recv.at[part, p])
        return remote(pieces.at[part, p], target, *sems, above[1] if p == 0 else below[p - 1])

    def own_copy(part):
        return pltpu.make_async_copy(pieces.at[part, 1], left_out.at[1, :, columns(part)], own_sem.at[part])

    def fresh_copy(part, q):
        target = right_out.at[q, columns(part)]
        return remote(fresh.at[part, q], target, fresh_send.at[part, q], fresh_recv.at[part, q], owner)

    def gate(p, q, n):
        inside = (middle >= p) & (middle + q < sectors)
        return jnp.where(inside, gate_ref[p * levels + q, n * levels + p + q - n], 0.0)

    def add_term(p, n):
        source = left_at(p, n)
        for q in range(levels):
            r = p + q - n
            if 0 <= r <= last:
                product = jnp.dot(source[...], right_in[q, last - r], preferred_element_type=jnp.float32)
                term = product.astype(jnp.bfloat16).astype(jnp.float32) * gate(p, q, n)
                if (p, q) in begun:
                    total[p, q] += term
                else:
                    total[p, q] = term
                    begun.add((p, q))

    def finish_row(p):
        for q in range(levels):
            block[p * size:(p + 1) * size, q * size:(q + 1) * size] = total[p, q].astype(jnp.bfloat16)
        row = block[p * size:(p + 1) * size, :]
        first = jnp.dot(row, test_in[...], preferred_element_type=jnp.float32).astype(jnp.bfloat16)
        back_total[...] += lax.dot_general(first, row, ROWS, preferred_element_type=jnp.float32)

    barrier = pltpu.get_barrier_semaphore()
    for partner in partners:
        pl.semaphore_signal(barrier, inc=1, device_id=partner, device_id_type=MESH)
    pl.semaphore_wait(barrier, len(partners))

    queue, here, queued, begun = [], set(), set(), set()
    terms_left = [levels] * levels

    def needs(p, n):
        offset = n - p
        slices = range(max(0, -offset), min(last, last - offset) + 1)
        return {("left", p, n)} | {("right", offset, r) for r in slices}

    def arrived(*what):
        here.add(what)
        for p in range(levels):
            for n in range(levels):
                if (p, n) not in queued and needs(p, n) <= here:
                    queued.add((p, n))
                    queue.append((p, n))

    def work_on(count):
        for _ in range(min(count, len(queue))):
            p, n = queue.pop(0)
            add_term(p, n)
            terms_left[p] -= 1
            if terms_left[p] == 0:
                finish_row(p)

    def left_steps(p, chunks):
        for n in chunks:
            left_copy(p, n).wait_recv()
            if 1 < p < last:
                left_copy(p + 1, n).start()
            arrived("left", p, n)
            work_on(2)

    def up_step(offset, r):
        up_copy(offset, r).wait_recv()
        if r > -offset:
            up_copy(offset - 1, r).start()
        arrived("right", offset, r)

    def down_step(offset, r):
        down_copy(offset, r).wait_recv()
        if r + offset < last:
            down_copy(offset + 1, r).start()
        arrived("right", offset, r)

    def right_steps(hop):
        for step in range(levels + 1 - hop):
            down_step(hop - 1, step)
            if hop < last and last - step > hop:
                up_step(-1 - hop, last - step)
            work_on(1)

    order = sorted(range(levels), key=lambda r: -max(r - 1, levels - r))
    for r in order:
        chain_copy(r).start()
    for n in range(levels):
        left_copy(2, n).start()
        left_copy(0, n).start()
        arrived("left", 1, n)
    kept_copy.start()
    back_total[...] = jnp.zeros_like(back_total)
    for r in order:
        chain_copy(r).wait_recv()
        down_copy(0, r).start()
        if r > 1:
            up_copy(-2, r).start()
        arrived("right", -1, r)
    for n in range(levels):
        left_steps(2, [n])
        left_steps(0, [n])
    right_steps(1)
    for n in range(levels):
        test_copy(n).start()
    for hop in range(2, last - 1):
        right_steps(hop)
        if hop == 3:
            for n in range(levels):
                test_copy(n).wait_recv()
        left_steps(hop + 1, range(levels))
    right_steps(last - 1)
    left_steps(last, range(levels // 3))
    right_steps(last)
    left_steps(last, range(levels // 3, 2 * levels // 3))
    right_steps(levels)
    left_steps(last, range(2 * levels // 3, levels))
    work_on(len(queue))
    kept_copy.wait_recv()

    back = back_total[...].astype(jnp.bfloat16)
    sketch[...] = lax.dot_general(block[...], back, COLUMNS, preferred_element_type=jnp.float32)
    scale = math.sqrt(levels * size)
    half = size // 2
    ridge = RIDGE_SHARE * jnp.sum(sketch[...] * sketch[...]) / size + TINY_SHIFT

    def load_gram(begin):
        gram = lax.dot_general(
            sketch[:, begin:begin + half], sketch[:, begin:], ROWS, precision=HIGHEST, preferred_element_type=jnp.float32
        )
        shape = (half, size - begin)
        work[begin:begin + half, begin:size] = gram + jnp.where(iota(shape, 0) == iota(shape, 1), ridge, 0.0)
        shape = (half, size)
        work[begin:begin + half, size:] = jnp.where(iota(shape, 0) + begin == iota(shape, 1), 1.0, 0.0)

    def send_pieces(part):
        begin = part * half
        basis = lax.dot_general(
            sketch[:, :begin + half], work[begin:begin + half, size:size + begin + half], COLUMNS,
            precision=HIGHEST, preferred_element_type=jnp.float32,
        )
        scaled = jnp.where(iota(basis.shape, 1) + begin < kept_in[0:1, :half], basis, 0.0) * scale
        for p in range(levels):
            pieces[part, p] = scaled[p * size:(p + 1) * size].astype(jnp.bfloat16)
        for p in (*range(last, 2, -1), 0, 2):
            piece_copy(part, p).start()
        own_copy(part).start()

    def send_fresh(part):
        scaled = pieces[part].reshape(levels * size, half)
        new_right = lax.dot_general(scaled, block[...], ROWS, preferred_element_type=jnp.float32) * (1.0 / scale)
        for q in range(levels):
            fresh[part, q] = new_right[:, q * size:(q + 1) * size].astype(jnp.bfloat16)
            fresh_copy(part, q).start()

    load_gram(0)
    invert_factor(min(64, half), work, 0, half)
    send_pieces(0)
    send_fresh(0)
    load_gram(half)
    top = work[:half, half:]
    work[half:, half:] -= lax.dot_general(
        top[:, :half], top, ROWS, precision=HIGHEST, preferred_element_type=jnp.float32
    )
    invert_factor(min(64, half), work, half, size)
    send_pieces(1)
    send_fresh(1)
    kept_copy.wait_send()
    for r in range(levels):
        chain_copy(r).wait_send()
        test_copy(r).wait_send()
        for p in range(levels):
            if p != 1:
                left_copy(p, r).wait_send()
        for offset in range(levels - r):
            down_copy(offset, r).wait_send()
        for offset in range(-r, -1):
            up_copy(offset, r).wait_send()
    for part in range(2):
        own_copy(part).wait()
        for q in range(levels):
            fresh_copy(part, q).wait()
        for p in range(levels):
            if p != 1:
                piece_copy(part, p).wait()


def run_layer(gates, kept, left, right, test_matrix, chains, sectors):
    levels, size = left.shape[0], left.shape[1]
    square = pltpu.SemaphoreType.DMA((levels, levels))
    scalar = pltpu.SemaphoreType.DMA
    one = pltpu.SemaphoreType.DMA((levels,))
    two = pltpu.SemaphoreType.DMA((2,))
    both = pltpu.SemaphoreType.DMA((2, levels))
    part = (levels, size, size)
    return pl.pallas_call(
        functools.partial(layer_kernel, levels, chains, sectors),
        out_shape=(jax.ShapeDtypeStruct(part, jnp.bfloat16), jax.ShapeDtypeStruct(part, jnp.bfloat16)),
        in_specs=[
            pl.BlockSpec(memory_space=pltpu.SMEM),
            pl.BlockSpec(memory_space=pltpu.VMEM),
            pl.BlockSpec(memory_space=pltpu.VMEM),
            pl.BlockSpec(memory_space=pl.ANY),
            pl.BlockSpec(memory_space=pl.ANY),
        ],
        out_specs=(pl.BlockSpec(memory_space=pl.ANY),) * 2,
        scratch_shapes=[
            pltpu.VMEM((levels * size, size), jnp.bfloat16),
            pltpu.VMEM(kept.shape, jnp.int32),
            pltpu.VMEM((levels, *part), jnp.bfloat16),
            pltpu.VMEM((levels, *part), jnp.bfloat16),
            pltpu.VMEM((size, size), jnp.bfloat16),
            pltpu.VMEM((levels, *part), jnp.float32),
            pltpu.VMEM((levels * size, levels * size), jnp.bfloat16),
            pltpu.VMEM((size, levels * size), jnp.float32),
            pltpu.VMEM((levels * size, size), jnp.float32),
            pltpu.VMEM((size, 2 * size), jnp.float32),
            pltpu.VMEM((2, levels, size, size // 2), jnp.bfloat16),
            pltpu.VMEM((2, levels, size // 2, size), jnp.bfloat16),
            one, one, one, one, scalar, scalar, square, square, square, square, square, square, both, both, both, both, two,
        ],
        compiler_params=pltpu.CompilerParams(
            collective_id=0, has_side_effects=True, vmem_limit_bytes=VMEM_LIMIT
        ),
    )(gates, kept, left, test_matrix, right)


def per_device(left_sites, right_sites, pair_gates, test_matrix, kept_columns):
    sectors = lax.axis_size("sector")
    sector = lax.axis_index("sector")
    chains = lax.axis_size("chain")
    chain = lax.axis_index("chain")
    left = jnp.transpose(left_sites[0, 0], (1, 0, 2))
    right = jnp.transpose(right_sites[0, 0], (1, 0, 2))
    gates = pair_gates[0].astype(jnp.float32)
    kept = jnp.broadcast_to(kept_columns, (8, 128))
    fresh_left, shipped = run_layer(gates, kept, left, right, test_matrix[0, 0], chains, sectors)
    inside = sector + jnp.arange(left.shape[0])[:, None, None] < sectors
    fresh_left = jnp.where(inside, fresh_left, jnp.zeros_like(fresh_left))
    new_left = jnp.where(chain == chains - 1, left, fresh_left)
    new_right = jnp.where(chain == 0, right, shipped)
    return (
        jnp.transpose(new_left, (1, 0, 2))[None, None],
        jnp.transpose(new_right, (1, 0, 2))[None, None],
    )


def solution(mesh):
    return jax.shard_map(
        per_device,
        mesh=mesh,
        in_specs=(
            P("chain", "sector", None, None, None),
            P("chain", "sector", None, None, None),
            P("chain", None, None),
            P("chain", "sector", None, None),
            P("chain", "sector"),
        ),
        out_specs=(P("chain", "sector", None, None, None), P("chain", "sector", None, None, None)),
        check_vma=False,
    )
```
